32 devices in a mesh: segment: 4 (over y, x), seq: 8 (over z, core).
Axes of the slice: x: 2, y: 2, z: 4, core: 2. Of those that a mesh axis runs over, the one named last changes fastest.
Arguments:
- sr_tokens: bfloat16 [8192, 2048], P('seq'), may hold values from -6 to 6
- base_latent: bfloat16 [512, 2048], P('seq'), may hold values from -6 to 6
- upsample_map: int32 [8192], P('seq'), may hold values from 0 to 511, as said below
- norm_gain: float32 [2048], replicated, may hold values from 0.1 to 1.9
- w_qkv: bfloat16 [3, 2048, 2048], P(None, None, 'segment'), may hold values from -0.125 to 0.125
- qk_gain: float32 [2, 2048], P(None, 'segment'), may hold values from 0.42 to 10.4
- w_out: bfloat16 [2048, 2048], P('segment'), may hold values from -0.5 to 0.5
- block_lists: int32 [128, 8], replicated, may hold values from 0 to 127, as said below
- block_counts: int32 [128], replicated, may hold values from 1 to 8
Outputs:
- updated: bfloat16 [8192, 2048], P('seq', 'segment')
The draws below stay inside these ranges and needn't reach their ends.
Inputs may be any that keep to these rules, and one draw needn't show every extreme that they name: upsample_map[t] names a low-resolution token whose frame, index // 64, differs by at most one from t // 1024. block_lists[b, 0] = b, and the entries of one row are distinct.
All inputs are finite; a program needn't handle non-finite values.
Results may differ from the reference program's by a relative error of at most 0.012.
The reference program's roundings to bfloat16 on the way count: a program that leaves them out, or rounds other values in their place, can miss the bound.
Values may be sent and summed in bfloat16 or wider, within the bound.
A program may use at most 128 MiB of HBM per device.

```python
import jax
import jax.numpy as jnp
from jax import lax

D = 2048
HEADS = 16
HD = 128
SIDE = 32
BASE_SIDE = 8
FRAME_TOK = 1024
BASE_FT = 64
SEQ_TOK = 8192
BASE_TOK = 512
BLOCK = 64
WINDOW = 8
QBLOCKS = 128


def draw_upsample_map(key, part):
    tok_index = jnp.arange(SEQ_TOK, dtype=jnp.int32)
    frame_index = tok_index // FRAME_TOK
    spot_index = tok_index % FRAME_TOK
    row_index = spot_index // SIDE
    col_index = spot_index % SIDE
    key_frame, key_row, key_col = jax.random.split(key, 3)
    frame_total = SEQ_TOK // FRAME_TOK
    factor = SIDE // BASE_SIDE
    base_frame = jnp.clip(frame_index + jax.random.randint(key_frame, (SEQ_TOK,), -1, 2), 0, frame_total - 1)
    base_row = jnp.clip(row_index // factor + jax.random.randint(key_row, (SEQ_TOK,), -1, 2), 0, BASE_SIDE - 1)
    base_col = jnp.clip(col_index // factor + jax.random.randint(key_col, (SEQ_TOK,), -1, 2), 0, BASE_SIDE - 1)
    return (base_frame * BASE_FT + base_row * BASE_SIDE + base_col).astype(jnp.int32)


def draw_block_lists(key, part):
    stride = QBLOCKS // WINDOW
    own_block = jnp.arange(QBLOCKS, dtype=jnp.int32)[:, None]
    steps_apart = jnp.arange(WINDOW, dtype=jnp.int32)[None, :] * stride
    jitter = jax.random.randint(key, (QBLOCKS, WINDOW), 1, stride)
    offsets = jnp.where(steps_apart == 0, 0, steps_apart + jitter)
    return ((own_block + offsets) % QBLOCKS).astype(jnp.int32)


def draw_block_counts(key, part):
    counts = jax.random.randint(key, (QBLOCKS,), 1, WINDOW + 1)
    return counts.at[0].set(WINDOW).astype(jnp.int32)


def draw_qk_gain(key, part):
    key_dims, key_heads = jax.random.split(key)
    per_dim = jax.random.uniform(key_dims, (2, HEADS, D // HEADS), jnp.float32, 0.7, 1.4)
    per_head = jnp.exp(jax.random.uniform(key_heads, (2, HEADS, 1), jnp.float32, -0.5, 0.7))
    return (per_dim * per_head).reshape(2, D).astype(jnp.float32)


def shard_levels(own_key, extent, shards, low, largest):
    loudness, own = 1.0, jax.random.fold_in(own_key, 6)
    for dim, parts in shards:
        steps = jnp.exp(jax.random.uniform(jax.random.fold_in(own, dim), (parts,), jnp.float32, low / len(shards), largest / len(shards)))
        loudness = loudness * jnp.repeat(steps, extent[dim] // parts).reshape([-1 if axis == dim else 1 for axis in range(len(extent))])
    return loudness


def normal_values(key, extent, spread, reach, cuts=(), kind=jnp.bfloat16):
    drawn = spread * jax.random.normal(key, extent, jnp.float32)
    if cuts:
        drawn = drawn * shard_levels(key, extent, cuts, -0.22, 0.18)
    return jnp.clip(drawn, -reach, reach).astype(kind)


def setup_inputs(seed: int = 0) -> dict:
    key_list = jax.random.split(jax.random.key(seed), 10)
    return {
        "sr_tokens": normal_values(key_list[0], (SEQ_TOK, D), 1.0, 6.0, ((0, 8),)),
        "base_latent": normal_values(key_list[1], (BASE_TOK, D), 1.0, 6.0, ((0, 8),)),
        "upsample_map": draw_upsample_map(jax.random.fold_in(key_list[9], 71), 0),
        "norm_gain": jnp.clip(1.0 + 0.18 * jax.random.normal(key_list[3], (D,), jnp.float32), 0.1, 1.9),
        "w_qkv": normal_values(key_list[4], (3, D, D), D ** -0.5, 0.125, ((2, 4),)),
        "qk_gain": draw_qk_gain(jax.random.fold_in(key_list[9], 71), 0),
        "w_out": normal_values(key_list[6], (D, D), (D // 16) ** -0.5, 0.5, ((0, 4),)),
        "block_lists": draw_block_lists(jax.random.fold_in(key_list[9], 71), 0),
        "block_counts": draw_block_counts(jax.random.fold_in(key_list[9], 71), 0),
    }


EPSILON = 1e-06

def rms_scale(tensor):
    return lax.rsqrt(lax.optimization_barrier(jnp.mean(tensor * tensor, axis=-1, keepdims=True)) + EPSILON)

def block_attend(query_blocks, key_rows, value_rows, block_lists, block_counts):
    head_dim = key_rows.shape[-1]
    key_blocks = key_rows.reshape(-1, BLOCK, head_dim)[block_lists]
    value_blocks = value_rows.reshape(-1, BLOCK, head_dim)[block_lists]
    scores = jnp.einsum('qbd,qwkd->qbwk', query_blocks.astype(jnp.float32), key_blocks.astype(jnp.float32)) * head_dim ** (-0.5)
    allowed = jnp.arange(block_lists.shape[1], dtype=jnp.int32)[None, :] < block_counts[:, None]
    scores = jnp.where(allowed[:, None, :, None], scores, -jnp.inf)
    row_top = lax.optimization_barrier(jnp.max(scores, axis=(2, 3), keepdims=True))
    weights = jnp.exp(scores - row_top)
    row_total = lax.optimization_barrier(jnp.sum(weights, axis=(2, 3)))
    prob_rows = weights.astype(jnp.bfloat16)
    summed = jnp.einsum('qbwk,qwkd->qbd', prob_rows.astype(jnp.float32), value_blocks.astype(jnp.float32))
    return (summed / row_total[:, :, None]).astype(jnp.bfloat16)

def reference(sr_tokens, base_latent, upsample_map, norm_gain, w_qkv, qk_gain, w_out, block_lists, block_counts):
    condition = base_latent[upsample_map]
    mixed_rows = sr_tokens.astype(jnp.float32) + condition.astype(jnp.float32)
    normed = (mixed_rows * rms_scale(mixed_rows) * norm_gain).astype(jnp.bfloat16)
    seq_len = normed.shape[0]
    raw_q = jnp.dot(normed, w_qkv[0], preferred_element_type=jnp.float32).reshape(seq_len, HEADS, HD)
    raw_k = jnp.dot(normed, w_qkv[1], preferred_element_type=jnp.float32).reshape(seq_len, HEADS, HD)
    raw_v = jnp.dot(normed, w_qkv[2], preferred_element_type=jnp.float32).reshape(seq_len, HEADS, HD)
    query_heads = (raw_q * rms_scale(raw_q) * qk_gain[0].reshape(HEADS, HD)).astype(jnp.bfloat16)
    key_heads = (raw_k * rms_scale(raw_k) * qk_gain[1].reshape(HEADS, HD)).astype(jnp.bfloat16)
    value_heads = raw_v.astype(jnp.bfloat16)
    query_stack = query_heads.transpose(1, 0, 2).reshape(HEADS, -1, BLOCK, HD)
    key_stack = key_heads.transpose(1, 0, 2)
    value_stack = value_heads.transpose(1, 0, 2)

    def one_head(operands):
        return block_attend(operands[0], operands[1], operands[2], block_lists, block_counts)
    attended = lax.map(one_head, (query_stack, key_stack, value_stack))
    attended = attended.reshape(HEADS, seq_len, HD).transpose(1, 0, 2).reshape(seq_len, HEADS * HD)
    projected = jnp.dot(attended, w_out, preferred_element_type=jnp.float32)
    return (mixed_rows + projected).astype(jnp.bfloat16)
```

```python
import functools

import jax
import jax.numpy as jnp
from jax import lax
from jax.experimental import pallas as pl
from jax.experimental.pallas import tpu as pltpu
from jax.sharding import PartitionSpec as P

HD = 128
BASE_FT = 64
BLOCK = 64
EPSILON = 1e-06
CHUNKS = 4
MESH = pl.DeviceIdType.MESH
MIB = 2**20


def padded_2(x, axis, width):
    count, length = lax.axis_size(axis), x.shape[0]
    up = [(i, (i + 1) % count) for i in range(count - 1)]
    down = [(j, i) for i, j in up]
    before = lax.ppermute(lax.slice_in_dim(x, length - width, length, axis=0), axis, up)
    after = lax.ppermute(lax.slice_in_dim(x, 0, width, axis=0), axis, down)
    return jnp.concatenate([before, x, after], axis=0)


def rms_scale(tensor):
    return lax.rsqrt(jnp.mean(tensor * tensor, axis=-1, keepdims=True) + EPSILON)


def front_kernel(heads, sr, base, place, gain, w_qkv, qk_gain, q_out, kv_out, share_out, mixed):
    rows = sr.shape[0]
    count = base.shape[0]
    hot = (lax.broadcasted_iota(jnp.int32, (rows, count), 1) == place[...]).astype(jnp.bfloat16)
    condition = jnp.dot(hot, base[...], preferred_element_type=jnp.float32)
    mixed[...] = sr[...].astype(jnp.float32) + condition
    width = share_out.shape[1]
    start = pl.multiple_of(lax.axis_index("segment") * width, width)
    share_out[...] = mixed[:, pl.ds(start, width)]
    whole = mixed[...]
    normed = (whole * rms_scale(whole) * gain[...]).astype(jnp.bfloat16)
    for which in range(3):
        raw = jnp.dot(normed, w_qkv[which], preferred_element_type=jnp.float32)
        for head in range(heads):
            cols = slice(head * HD, (head + 1) * HD)
            part = raw[:, cols]
            if which < 2:
                part = part * rms_scale(part) * qk_gain[which : which + 1, cols]
            part = part.astype(jnp.bfloat16)
            if which == 0:
                q_out[head] = part
            else:
                kv_out[head, which - 1] = part


def front(sr, base, place, gain, w_qkv, qk_gain):
    rows, depth = sr.shape
    width = w_qkv.shape[2]
    heads = width // HD
    tile = 256
    share = depth // lax.axis_size("segment")
    return pl.pallas_call(
        functools.partial(front_kernel, heads),
        grid=(rows // tile,),
        in_specs=[
            pl.BlockSpec((tile, depth), lambda i: (i, 0)),
            pl.BlockSpec(base.shape, lambda i: (0, 0)),
            pl.BlockSpec((tile, 1), lambda i: (i, 0)),
            pl.BlockSpec((1, depth), lambda i: (0, 0)),
            pl.BlockSpec(w_qkv.shape, lambda i: (0, 0, 0)),
            pl.BlockSpec(qk_gain.shape, lambda i: (0, 0)),
        ],
        out_specs=[
            pl.BlockSpec((heads, tile, HD), lambda i: (0, i, 0)),
            pl.BlockSpec((heads, 2, tile, HD), lambda i: (0, 0, i, 0)),
            pl.BlockSpec((tile, share), lambda i: (i, 0)),
        ],
        out_shape=[
            jax.ShapeDtypeStruct((heads, rows, HD), jnp.bfloat16),
            jax.ShapeDtypeStruct((heads, 2, rows, HD), jnp.bfloat16),
            jax.ShapeDtypeStruct((rows, share), jnp.float32),
        ],
        scratch_shapes=[pltpu.VMEM((tile, depth), jnp.float32)],
        compiler_params=pltpu.CompilerParams(vmem_limit_bytes=48 * MIB),
        name="front",
    )(sr, base, place, gain, w_qkv, qk_gain)


def greet(targets):
    barrier = pltpu.get_barrier_semaphore()
    for target in targets:
        pl.semaphore_signal(barrier, inc=1, device_id=target, device_id_type=MESH)
    pl.semaphore_wait(barrier, len(targets))


def remote(src, dst, send, recv, target):
    return pltpu.make_async_remote_copy(
        src_ref=src, dst_ref=dst, send_sem=send, recv_sem=recv, device_id=target, device_id_type=MESH
    )


def exchange_kernel(
    seqs, segs, groups, q, kv, w_out, kv_all, q_all, w_cols,
    kv_send, kv_recv, q_send, q_recv, fw_send, fw_recv, w_send, w_recv, own,
):
    me, seg = lax.axis_index("seq"), lax.axis_index("segment")
    rows = q.shape[1]
    part_rows = rows // groups
    head, part = me // groups, me % groups
    depth, share = w_out.shape[0], w_out.shape[1] // segs
    greet(
        [(seg, lax.rem(me + k, seqs)) for k in range(1, seqs)]
        + [(lax.rem(seg + k, segs), me) for k in range(1, segs)]
    )

    def rows_of(which):
        return pl.ds(pl.multiple_of(which * part_rows, part_rows), part_rows)

    def landing(source, which):
        start = pl.multiple_of(source * rows + which * part_rows, part_rows)
        return kv_all.at[:, pl.ds(start, part_rows), :]

    def kv_copy(target, source):
        return remote(
            kv.at[target // groups, :, rows_of(target % groups), :],
            landing(source, target % groups),
            kv_send.at[target],
            kv_recv.at[source],
            (seg, target),
        )

    def q_copy(target, source):
        return remote(
            q.at[target // groups, rows_of(target % groups), :],
            q_all.at[source],
            q_send.at[target],
            q_recv.at[source],
            (seg, target),
        )

    def w_copy(target, source):
        return remote(
            w_out.at[:, pl.ds(pl.multiple_of(target * share, share), share)],
            w_cols.at[pl.ds(pl.multiple_of(source * depth, depth), depth), :],
            w_send.at[target],
            w_recv.at[source],
            (target, me),
        )

    def forward(source, step, sender_part):
        slot = landing(source, sender_part)
        target = head * groups + lax.rem(part + step, groups)
        return remote(
            slot, slot, fw_send.at[source, step - 1], fw_recv.at[source, step - 1], (seg, target)
        )

    own_kv = pltpu.make_async_copy(kv.at[head, :, rows_of(part), :], landing(me, part), own.at[0])
    own_q = pltpu.make_async_copy(q.at[head, rows_of(part), :], q_all.at[me], own.at[1])
    own_w = pltpu.make_async_copy(
        w_out.at[:, pl.ds(pl.multiple_of(seg * share, share), share)],
        w_cols.at[pl.ds(pl.multiple_of(seg * depth, depth), depth), :],
        own.at[2],
    )
    own_kv.start()

    @pl.loop(1, seqs)
    def _(k):
        kv_copy(lax.rem(me + k, seqs), me).start()

    @pl.loop(1, seqs)
    def _(k):
        q_copy(lax.rem(me + k, seqs), me).start()

    own_q.start()
    own_w.start()

    @pl.loop(1, segs)
    def _(k):
        w_copy(lax.rem(seg + k, segs), seg).start()

    own_kv.wait()
    for step in range(1, groups):
        forward(me, step, part).start()

    @pl.loop(1, seqs)
    def _(k):
        source = lax.rem(me + seqs - k, seqs)
        kv_copy(me, source).wait_recv()
        for step in range(1, groups):
            forward(source, step, part).start()

    @pl.loop(0, seqs)
    def _(k):
        source = lax.rem(me + k, seqs)
        for step in range(1, groups):
            forward(source, step, lax.rem(part + groups - step, groups)).wait_recv()
            forward(source, step, part).wait_send()

    @pl.loop(1, seqs)
    def _(k):
        q_copy(me, lax.rem(me + seqs - k, seqs)).wait_recv()
        target = lax.rem(me + k, seqs)
        kv_copy(target, me).wait_send()
        q_copy(target, me).wait_send()

    @pl.loop(1, segs)
    def _(k):
        w_copy(seg, lax.rem(seg + segs - k, segs)).wait_recv()
        w_copy(lax.rem(seg + k, segs), seg).wait_send()

    own_q.wait()
    own_w.wait()


def exchange(q, kv, w_out, seqs, segs, groups):
    heads, rows, _ = q.shape
    depth, width = w_out.shape
    dma = pltpu.SemaphoreType.DMA
    anywhere = pl.BlockSpec(memory_space=pl.ANY)
    return pl.pallas_call(
        functools.partial(exchange_kernel, seqs, segs, groups),
        in_specs=[anywhere] * 3,
        out_specs=[anywhere] * 3,
        out_shape=[
            jax.ShapeDtypeStruct((2, seqs * rows, HD), jnp.bfloat16),
            jax.ShapeDtypeStruct((seqs, rows // groups, HD), jnp.bfloat16),
            jax.ShapeDtypeStruct((segs * depth, width // segs), jnp.bfloat16),
        ],
        scratch_shapes=[
            dma((seqs,)), dma((seqs,)), dma((seqs,)), dma((seqs,)),
            dma((seqs, max(groups - 1, 1))), dma((seqs, max(groups - 1, 1))),
            dma((segs,)), dma((segs,)), dma((3,)),
        ],
        compiler_params=pltpu.CompilerParams(collective_id=0, has_side_effects=True),
        name="exchange",
    )(q, kv, w_out)


def attend_kernel(blocks_source, blocks_part, groups, together, lists, counts, q, kv, out):
    window = lists.shape[0] // counts.shape[0]
    first = (lax.axis_index("seq") % groups) * blocks_part
    span = window * BLOCK
    column = lax.broadcasted_iota(jnp.int32, (BLOCK, span), 1)

    def one(index):
        block = (index // blocks_part) * blocks_source + first + index % blocks_part
        starts = [pl.multiple_of(lists[block * window + w] * BLOCK, BLOCK) for w in range(window)]
        keys = jnp.concatenate([kv[0, pl.ds(at, BLOCK), :] for at in starts], axis=0)
        values = jnp.concatenate([kv[1, pl.ds(at, BLOCK), :] for at in starts], axis=0)
        query = q[pl.ds(pl.multiple_of(index * BLOCK, BLOCK), BLOCK), :]
        scores = lax.dot_general(
            query, keys, (((1,), (1,)), ((), ())), preferred_element_type=jnp.float32
        ) * HD ** (-0.5)
        scores = jnp.where(column < counts[block] * BLOCK, scores, -jnp.inf)
        weights = jnp.exp(scores - jnp.max(scores, axis=1, keepdims=True))
        total = jnp.sum(weights, axis=1, keepdims=True)
        summed = jnp.dot(weights.astype(jnp.bfloat16), values, preferred_element_type=jnp.float32)
        return (summed / total).astype(jnp.bfloat16)

    @pl.loop(0, out.shape[0] // (BLOCK * together))
    def _(step):
        done = [one(step * together + i) for i in range(together)]
        for i in range(together):
            at = pl.multiple_of((step * together + i) * BLOCK, BLOCK)
            out[pl.ds(at, BLOCK), :] = done[i]


def attend(lists, counts, q, kv, blocks_source, groups):
    blocks_part = blocks_source // groups
    return pl.pallas_call(
        functools.partial(attend_kernel, blocks_source, blocks_part, groups, 4),
        in_specs=[pl.BlockSpec(memory_space=pltpu.SMEM)] * 2
        + [pl.BlockSpec(memory_space=pltpu.VMEM)] * 2,
        out_specs=pl.BlockSpec(memory_space=pltpu.VMEM),
        out_shape=jax.ShapeDtypeStruct(q.shape, jnp.bfloat16),
        compiler_params=pltpu.CompilerParams(vmem_limit_bytes=48 * MIB),
        name="attend",
    )(lists, counts, q, kv)


def finish_kernel(
    seqs, groups, chunks, att, w_cols, share, out, full, z_send, z_recv, p_send, p_recv, own,
):
    me, seg = lax.axis_index("seq"), lax.axis_index("segment")
    head, part = me // groups, me % groups
    part_rows = att.shape[1]
    size = part_rows // chunks
    half = size // 2
    width = full.shape[3]
    near_x, near_y = seg ^ 1, seg ^ 2
    greet(
        [(seg, lax.rem(me + k, seqs)) for k in range(1, seqs)] + [(near_x, me), (near_y, me)]
    )

    def spot(chunk, owner):
        lanes = pl.ds(pl.multiple_of((owner // groups) * HD, HD), HD)
        return full.at[seg, owner % groups, pl.ds(pl.multiple_of(chunk * size, size), size), lanes]

    def z_copy(chunk, target, owner):
        return remote(
            att.at[target, pl.ds(pl.multiple_of(chunk * size, size), size), :],
            spot(chunk, owner),
            z_send.at[chunk, target],
            z_recv.at[chunk, owner],
            (seg, target),
        )

    def own_copy(chunk):
        return pltpu.make_async_copy(
            att.at[me, pl.ds(pl.multiple_of(chunk * size, size), size), :],
            spot(chunk, me),
            own.at[chunk],
        )

    def pair_copy(chunk, kind, origin, to):
        at = pl.multiple_of(chunk * size + (half if kind == 3 else 0), half)
        piece = full.at[origin, :, pl.ds(at, size if kind < 2 else half), :]
        return remote(piece, piece, p_send.at[chunk, kind], p_recv.at[chunk, kind], (to, me))

    @pl.loop(0, chunks)
    def _(chunk):
        own_copy(chunk).start()

        @pl.loop(1, seqs)
        def _(k):
            z_copy(chunk, lax.rem(me + k, seqs), me).start()

    @pl.loop(0, chunks + 2)
    def _(step):
        @pl.when(step < chunks)
        def _():
            own_copy(step).wait()

            @pl.loop(1, seqs)
            def _(k):
                z_copy(step, me, lax.rem(me + seqs - k, seqs)).wait_recv()

            pair_copy(step, 0, seg, near_x).start()
            pair_copy(step, 1, seg, near_y).start()

        @pl.when(jnp.logical_and(step >= 1, step < chunks + 1))
        def _():
            chunk = step - 1
            pair_copy(chunk, 0, near_x, near_x).wait_recv()
            pair_copy(chunk, 2, near_x, near_y).start()
            pair_copy(chunk, 1, near_y, near_y).wait_recv()
            pair_copy(chunk, 3, near_y, near_x).start()

        @pl.when(step >= 2)
        def _():
            chunk = step - 2
            far = seg ^ 3
            pair_copy(chunk, 2, far, near_y).wait_recv()
            pair_copy(chunk, 3, far, near_x).wait_recv()
            rows = pl.ds(pl.multiple_of(chunk * size, size), size)
            total = jnp.zeros((groups * size, out.shape[2]), jnp.float32)
            for j in range(full.shape[0]):
                piece = full[j, :, rows, :].reshape(groups * size, width)
                total += jnp.dot(
                    piece, w_cols[j * width : (j + 1) * width, :], preferred_element_type=jnp.float32
                )
            total = total.reshape(groups, size, out.shape[2])
            out[:, rows, :] = (share[:, rows, :] + total).astype(jnp.bfloat16)

    @pl.loop(0, chunks)
    def _(chunk):
        pair_copy(chunk, 0, seg, near_x).wait_send()
        pair_copy(chunk, 1, seg, near_y).wait_send()
        pair_copy(chunk, 2, near_x, near_y).wait_send()
        pair_copy(chunk, 3, near_y, near_x).wait_send()

        @pl.loop(1, seqs)
        def _(k):
            z_copy(chunk, lax.rem(me + k, seqs), me).wait_send()


def finish(att, w_cols, share, seqs, segs, groups):
    part_rows = att.shape[1]
    width = w_cols.shape[0] // segs
    cols = w_cols.shape[1]
    dma = pltpu.SemaphoreType.DMA
    vmem = pl.BlockSpec(memory_space=pltpu.VMEM)
    return pl.pallas_call(
        functools.partial(finish_kernel, seqs, groups, CHUNKS),
        in_specs=[vmem] * 3,
        out_specs=vmem,
        out_shape=jax.ShapeDtypeStruct((groups, part_rows, cols), jnp.bfloat16),
        scratch_shapes=[
            pltpu.VMEM((segs, groups, part_rows, width), jnp.bfloat16),
            dma((CHUNKS, seqs)), dma((CHUNKS, seqs)), dma((CHUNKS, 4)), dma((CHUNKS, 4)),
            dma((CHUNKS,)),
        ],
        compiler_params=pltpu.CompilerParams(
            collective_id=1, has_side_effects=True, vmem_limit_bytes=48 * MIB
        ),
        name="finish",
    )(att, w_cols, share)


def on_device(
    sr_tokens, base_latent, upsample_map, norm_gain, w_qkv, qk_gain, w_out, block_lists, block_counts
):
    seqs, segs = lax.axis_size("seq"), lax.axis_size("segment")
    rank = lax.axis_index("seq")
    rows = sr_tokens.shape[0]
    heads = w_qkv.shape[2] // HD
    groups = seqs // heads
    part_rows = rows // groups
    padded = padded_2(base_latent, "seq", BASE_FT)
    place = (upsample_map - (rank * base_latent.shape[0] - BASE_FT))[:, None]
    q, kv, share = front(sr_tokens, padded, place, norm_gain[None], w_qkv, qk_gain)
    kv_all, q_all, w_cols = exchange(q, kv, w_out, seqs, segs, groups)
    att = attend(
        block_lists.reshape(-1), block_counts, q_all.reshape(-1, HD), kv_all, rows // BLOCK, groups
    )
    out = finish(
        att.reshape(seqs, part_rows, HD), w_cols, share.reshape(groups, part_rows, -1), seqs, segs, groups
    )
    return out.reshape(rows, -1)


def solution(mesh):
    placed = (
        P("seq", None),
        P("seq", None),
        P("seq"),
        P(),
        P(None, None, "segment"),
        P(None, "segment"),
        P("segment", None),
        P(),
        P(),
    )
    return jax.shard_map(
        on_device, mesh=mesh, in_specs=placed, out_specs=P("seq", "segment"), check_vma=False
    )
```

```python
import functools

import jax
import jax.numpy as jnp
from jax import lax
from jax.experimental import pallas as pl
from jax.experimental.pallas import tpu as pltpu
from jax.sharding import PartitionSpec as P

HD = 128
BASE_FT = 64
BLOCK = 64
EPSILON = 1e-06
CHUNKS = 4
TOGETHER = 4
MESH = pl.DeviceIdType.MESH
MIB = 2**20


def padded_2(x, axis, width):
    count, length = lax.axis_size(axis), x.shape[0]
    up = [(i, (i + 1) % count) for i in range(count - 1)]
    down = [(j, i) for i, j in up]
    before = lax.ppermute(lax.slice_in_dim(x, length - width, length, axis=0), axis, up)
    after = lax.ppermute(lax.slice_in_dim(x, 0, width, axis=0), axis, down)
    return jnp.concatenate([before, x, after], axis=0)


def rms_scale(tensor):
    return lax.rsqrt(jnp.mean(tensor * tensor, axis=-1, keepdims=True) + EPSILON)


def front_kernel(heads, sr, base, place, gain, w_qkv, qk_gain, q_out, kv_out, share_out, mixed):
    rows = sr.shape[0]
    count = base.shape[0]
    hot = (lax.broadcasted_iota(jnp.int32, (rows, count), 1) == place[...]).astype(jnp.bfloat16)
    condition = jnp.dot(hot, base[...], preferred_element_type=jnp.float32)
    mixed[...] = sr[...].astype(jnp.float32) + condition
    width = share_out.shape[1]
    start = pl.multiple_of(lax.axis_index("segment") * width, width)
    share_out[...] = mixed[:, pl.ds(start, width)]
    whole = mixed[...]
    normed = (whole * rms_scale(whole) * gain[...]).astype(jnp.bfloat16)
    for which in range(3):
        raw = jnp.dot(normed, w_qkv[which], preferred_element_type=jnp.float32)
        for head in range(heads):
            cols = slice(head * HD, (head + 1) * HD)
            part = raw[:, cols]
            if which < 2:
                part = part * rms_scale(part) * qk_gain[which : which + 1, cols]
            part = part.astype(jnp.bfloat16)
            if which == 0:
                q_out[head] = part
            else:
                kv_out[head, which - 1] = part


def front(sr, base, place, gain, w_qkv, qk_gain):
    rows, depth = sr.shape
    width = w_qkv.shape[2]
    heads = width // HD
    tile = 256
    share = depth // lax.axis_size("segment")
    return pl.pallas_call(
        functools.partial(front_kernel, heads),
        grid=(rows // tile,),
        in_specs=[
            pl.BlockSpec((tile, depth), lambda i: (i, 0)),
            pl.BlockSpec(base.shape, lambda i: (0, 0)),
            pl.BlockSpec((tile, 1), lambda i: (i, 0)),
            pl.BlockSpec((1, depth), lambda i: (0, 0)),
            pl.BlockSpec(w_qkv.shape, lambda i: (0, 0, 0)),
            pl.BlockSpec(qk_gain.shape, lambda i: (0, 0)),
        ],
        out_specs=[
            pl.BlockSpec((heads, tile, HD), lambda i: (0, i, 0)),
            pl.BlockSpec((heads, 2, tile, HD), lambda i: (0, 0, i, 0)),
            pl.BlockSpec((tile, share), lambda i: (i, 0)),
        ],
        out_shape=[
            jax.ShapeDtypeStruct((heads, rows, HD), jnp.bfloat16),
            jax.ShapeDtypeStruct((heads, 2, rows, HD), jnp.bfloat16),
            jax.ShapeDtypeStruct((rows, share), jnp.float32),
        ],
        scratch_shapes=[pltpu.VMEM((tile, depth), jnp.float32)],
        compiler_params=pltpu.CompilerParams(vmem_limit_bytes=48 * MIB),
        name="front",
    )(sr, base, place, gain, w_qkv, qk_gain)


def greet(targets):
    barrier = pltpu.get_barrier_semaphore()
    for target in targets:
        pl.semaphore_signal(barrier, inc=1, device_id=target, device_id_type=MESH)
    pl.semaphore_wait(barrier, len(targets))


def remote(src, dst, send, recv, target):
    return pltpu.make_async_remote_copy(
        src_ref=src, dst_ref=dst, send_sem=send, recv_sem=recv, device_id=target, device_id_type=MESH
    )


def middle_kernel(
    seqs, segs, groups, chunks, together,
    lists, counts, q, kv, w_out, share, out,
    kv_all, q_all, att, full, w_cols,
    kv_send, kv_recv, q_send, q_recv, fw_send, fw_recv, w_send, w_recv,
    z_send, z_recv, p_send, p_recv, own, own_chunk,
):
    me, seg = lax.axis_index("seq"), lax.axis_index("segment")
    rows = q.shape[1]
    part_rows = rows // groups
    size = part_rows // chunks
    half = size // 2
    head, part = me // groups, me % groups
    depth, cols = w_out.shape[0], w_out.shape[1] // segs
    window = lists.shape[0] // counts.shape[0]
    near_x, near_y, far = seg ^ 1, seg ^ 2, seg ^ 3
    greet([(seg, me ^ k) for k in range(1, seqs)] + [(seg ^ k, me) for k in range(1, segs)])

    blocks_source, blocks_part, blocks_chunk = rows // BLOCK, part_rows // BLOCK, size // BLOCK

    def blocks_of(which):
        return pl.ds(which * blocks_part, blocks_part)

    def chunk_rows(chunk):
        return pl.ds(pl.multiple_of(chunk * size, size), size)

    def landing(source, which):
        start = source * blocks_source + which * blocks_part
        return kv_all.at[:, pl.ds(start, blocks_part)]

    def kv_copy(target, source):
        return remote(
            kv.at[target // groups, :, blocks_of(target % groups)],
            landing(source, target % groups),
            kv_send.at[target],
            kv_recv.at[source],
            (seg, target),
        )

    def q_from(chunk, target):
        start = pl.multiple_of((target % groups) * part_rows + chunk * size, size)
        return q.at[target // groups, pl.ds(start, size), :]

    def q_copy(chunk, target, source):
        return remote(
            q_from(chunk, target),
            q_all.at[source, chunk_rows(chunk), :],
            q_send.at[chunk, target],
            q_recv.at[chunk, source],
            (seg, target),
        )

    def w_from(target):
        return w_out.at[:, pl.ds(pl.multiple_of(target * cols, cols), cols)]

    def w_to(source):
        return w_cols.at[pl.ds(pl.multiple_of(source * depth, depth), depth), :]

    def w_copy(target, source):
        return remote(
            w_from(target), w_to(source), w_send.at[target], w_recv.at[source], (target, me)
        )

    def forward(source, step, sender_part):
        slot = landing(source, sender_part)
        target = head * groups + lax.rem(part + step, groups)
        return remote(
            slot, slot, fw_send.at[source, step - 1], fw_recv.at[source, step - 1], (seg, target)
        )

    def spot(chunk, owner):
        lanes = pl.ds(pl.multiple_of((owner // groups) * HD, HD), HD)
        return full.at[seg, owner % groups, chunk_rows(chunk), lanes]

    def z_copy(chunk, target, owner):
        return remote(
            att.at[target, chunk_rows(chunk), :],
            spot(chunk, owner),
            z_send.at[chunk, target],
            z_recv.at[chunk, owner],
            (seg, target),
        )

    def own_copy(chunk):
        return pltpu.make_async_copy(
            att.at[me, chunk_rows(chunk), :], spot(chunk, me), own_chunk.at[chunk]
        )

    def pair_copy(chunk, kind, origin, to):
        at = pl.multiple_of(chunk * size + (half if kind == 3 else 0), half)
        piece = full.at[origin, :, pl.ds(at, size if kind < 2 else half), :]
        return remote(piece, piece, p_send.at[chunk, kind], p_recv.at[chunk, kind], (to, me))

    own_kv = pltpu.make_async_copy(kv.at[head, :, blocks_of(part)], landing(me, part), own.at[0])
    own_q = pltpu.make_async_copy(
        q.at[head, pl.ds(pl.multiple_of(part * part_rows, part_rows), part_rows), :], q_all.at[me], own.at[1]
    )
    own_w = pltpu.make_async_copy(w_from(seg), w_to(seg), own.at[2])
    own_kv.start()

    @pl.loop(1, seqs)
    def _(k):
        kv_copy(me ^ (seqs - k), me).start()

    own_q.start()
    own_w.start()

    @pl.loop(1, segs)
    def _(k):
        w_copy(seg ^ k, seg).start()

    own_kv.wait()
    for step in range(1, groups):
        forward(me, step, part).start()

    @pl.loop(1, seqs)
    def _(k):
        other = me ^ k
        kv_copy(me, other).wait_recv()
        for step in range(1, groups):
            forward(other, step, part).start()
        kv_copy(other, me).wait_send()

        @pl.loop(0, chunks)
        def _(chunk):
            q_copy(chunk, other, me).start()

    @pl.loop(0, seqs)
    def _(source):
        for step in range(1, groups):
            forward(source, step, lax.rem(part + groups - step, groups)).wait_recv()
            forward(source, step, part).wait_send()

    own_q.wait()

    column = lax.broadcasted_iota(jnp.int32, (BLOCK, window * BLOCK), 1)

    def one(source, local):
        block = source * blocks_source + part * blocks_part + local
        listed = [lists[block * window + w] for w in range(window)]
        keys = jnp.concatenate([kv_all[0, at] for at in listed], axis=0)
        values = jnp.concatenate([kv_all[1, at] for at in listed], axis=0)
        query = q_all[source, pl.ds(pl.multiple_of(local * BLOCK, BLOCK), BLOCK), :]
        scores = lax.dot_general(
            query, keys, (((1,), (1,)), ((), ())), preferred_element_type=jnp.float32
        ) * HD ** (-0.5)
        scores = jnp.where(column < counts[block] * BLOCK, scores, -jnp.inf)
        weights = jnp.exp(scores - jnp.max(scores, axis=1, keepdims=True))
        total = jnp.sum(weights, axis=1, keepdims=True)
        summed = jnp.dot(weights.astype(jnp.bfloat16), values, preferred_element_type=jnp.float32)
        return (summed / total).astype(jnp.bfloat16)

    def attend(chunk):
        @pl.loop(0, seqs * blocks_chunk // together)
        def _(step):
            places = []
            for i in range(together):
                index = step * together + i
                places.append((index // blocks_chunk, chunk * blocks_chunk + index % blocks_chunk))
            done = [one(*place) for place in places]
            for (source, local), value in zip(places, done):
                att[source, pl.ds(pl.multiple_of(local * BLOCK, BLOCK), BLOCK), :] = value

    @pl.loop(0, chunks + 3)
    def _(step):
        @pl.when(step < chunks)
        def _():
            @pl.loop(1, seqs)
            def _(k):
                q_copy(step, me, me ^ k).wait_recv()

            attend(step)

            @pl.loop(1, seqs)
            def _(k):
                z_copy(step, me ^ (seqs - k), me).start()

            own_copy(step).start()

        @pl.when(jnp.logical_and(step >= 1, step < chunks + 1))
        def _():
            chunk = step - 1
            own_copy(chunk).wait()

            @pl.loop(1, seqs)
            def _(k):
                z_copy(chunk, me, me ^ k).wait_recv()

            pair_copy(chunk, 0, seg, near_x).start()
            pair_copy(chunk, 1, seg, near_y).start()

        @pl.when(jnp.logical_and(step >= 2, step < chunks + 2))
        def _():
            chunk = step - 2
            pair_copy(chunk, 0, near_x, near_x).wait_recv()
            pair_copy(chunk, 2, near_x, near_y).start()
            pair_copy(chunk, 1, near_y, near_y).wait_recv()
            pair_copy(chunk, 3, near_y, near_x).start()

        @pl.when(step == 3)
        def _():
            own_w.wait()

            @pl.loop(1, segs)
            def _(k):
                w_copy(seg, seg ^ k).wait_recv()

        @pl.when(step >= 3)
        def _():
            chunk = step - 3
            pair_copy(chunk, 2, far, near_y).wait_recv()
            pair_copy(chunk, 3, far, near_x).wait_recv()
            here = chunk_rows(chunk)
            total = jnp.zeros((groups * size, cols), jnp.float32)
            for j in range(segs):
                piece = full[j, :, here, :].reshape(groups * size, depth)
                total += jnp.dot(
                    piece, w_cols[j * depth : (j + 1) * depth, :], preferred_element_type=jnp.float32
                )
            total = total.reshape(groups, size, cols)
            out[:, here, :] = (share[:, here, :] + total).astype(jnp.bfloat16)

    @pl.loop(0, chunks)
    def _(chunk):
        pair_copy(chunk, 0, seg, near_x).wait_send()
        pair_copy(chunk, 1, seg, near_y).wait_send()
        pair_copy(chunk, 2, near_x, near_y).wait_send()
        pair_copy(chunk, 3, near_y, near_x).wait_send()

        @pl.loop(1, seqs)
        def _(k):
            q_copy(chunk, me ^ k, me).wait_send()
            z_copy(chunk, me ^ k, me).wait_send()

    @pl.loop(1, segs)
    def _(k):
        w_copy(seg ^ k, seg).wait_send()


def middle(lists, counts, q, kv, w_out, share, seqs, segs, groups):
    heads, rows, _ = q.shape
    depth, width = w_out.shape
    part_rows = rows // groups
    chunks = min(CHUNKS, part_rows // BLOCK)
    cols = width // segs
    dma = pltpu.SemaphoreType.DMA
    anywhere = pl.BlockSpec(memory_space=pl.ANY)
    vmem = pl.BlockSpec(memory_space=pltpu.VMEM)
    smem = pl.BlockSpec(memory_space=pltpu.SMEM)
    return pl.pallas_call(
        functools.partial(middle_kernel, seqs, segs, groups, chunks, TOGETHER),
        in_specs=[smem, smem, anywhere, anywhere, anywhere, vmem],
        out_specs=vmem,
        out_shape=jax.ShapeDtypeStruct((groups, part_rows, cols), jnp.bfloat16),
        scratch_shapes=[
            pltpu.VMEM((2, seqs * rows // BLOCK, BLOCK, HD), jnp.bfloat16),
            pltpu.VMEM((seqs, part_rows, HD), jnp.bfloat16),
            pltpu.VMEM((seqs, part_rows, HD), jnp.bfloat16),
            pltpu.VMEM((segs, groups, part_rows, depth), jnp.bfloat16),
            pltpu.VMEM((segs * depth, cols), jnp.bfloat16),
            dma((seqs,)), dma((seqs,)), dma((chunks, seqs)), dma((chunks, seqs)),
            dma((seqs, max(groups - 1, 1))), dma((seqs, max(groups - 1, 1))),
            dma((segs,)), dma((segs,)),
            dma((chunks, seqs)), dma((chunks, seqs)), dma((chunks, 4)), dma((chunks, 4)),
            dma((3,)), dma((chunks,)),
        ],
        compiler_params=pltpu.CompilerParams(
            collective_id=0, has_side_effects=True, vmem_limit_bytes=48 * MIB
        ),
        name="middle",
    )(lists, counts, q, kv.reshape(heads, 2, rows // BLOCK, BLOCK, HD), w_out, share)


def on_device(
    sr_tokens, base_latent, upsample_map, norm_gain, w_qkv, qk_gain, w_out, block_lists, block_counts
):
    seqs, segs = lax.axis_size("seq"), lax.axis_size("segment")
    rank = lax.axis_index("seq")
    rows = sr_tokens.shape[0]
    heads = w_qkv.shape[2] // HD
    groups = seqs // heads
    part_rows = rows // groups
    padded = padded_2(base_latent, "seq", BASE_FT)
    place = (upsample_map - (rank * base_latent.shape[0] - BASE_FT))[:, None]
    q, kv, share = front(sr_tokens, padded, place, norm_gain[None], w_qkv, qk_gain)
    out = middle(
        block_lists.reshape(-1), block_counts, q, kv, w_out,
        share.reshape(groups, part_rows, -1), seqs, segs, groups,
    )
    return out.reshape(rows, -1)


def solution(mesh):
    placed = (
        P("seq", None),
        P("seq", None),
        P("seq"),
        P(),
        P(None, None, "segment"),
        P(None, "segment"),
        P("segment", None),
        P(),
        P(),
    )
    return jax.shard_map(
        on_device, mesh=mesh, in_specs=placed, out_specs=P("seq", "segment"), check_vma=False
    )
```

```python
import functools

import jax
import jax.numpy as jnp
from jax import lax
from jax.experimental import pallas as pl
from jax.experimental.pallas import tpu as pltpu
from jax.sharding import PartitionSpec as P

HD = 128
BASE_FT = 64
BLOCK = 64
EPSILON = 1e-06
CHUNKS = 8
TOGETHER = 4
MESH = pl.DeviceIdType.MESH
MIB = 2**20


def padded_2(x, axis, width):
    count, length = lax.axis_size(axis), x.shape[0]
    up = [(i, (i + 1) % count) for i in range(count - 1)]
    down = [(j, i) for i, j in up]
    before = lax.ppermute(lax.slice_in_dim(x, length - width, length, axis=0), axis, up)
    after = lax.ppermute(lax.slice_in_dim(x, 0, width, axis=0), axis, down)
    return jnp.concatenate([before, x, after], axis=0)


def rms_scale(tensor):
    return lax.rsqrt(jnp.mean(tensor * tensor, axis=-1, keepdims=True) + EPSILON)


def front_kernel(heads, sr, base, place, gain, w_qkv, qk_gain, q_out, kv_out, share_out, mixed):
    rows = sr.shape[0]
    count = base.shape[0]
    hot = (lax.broadcasted_iota(jnp.int32, (rows, count), 1) == place[...]).astype(jnp.bfloat16)
    condition = jnp.dot(hot, base[...], preferred_element_type=jnp.float32)
    mixed[...] = sr[...].astype(jnp.float32) + condition
    width = share_out.shape[1]
    start = pl.multiple_of(lax.axis_index("segment") * width, width)
    share_out[...] = mixed[:, pl.ds(start, width)]
    whole = mixed[...]
    normed = (whole * rms_scale(whole) * gain[...]).astype(jnp.bfloat16)
    for which in range(3):
        raw = jnp.dot(normed, w_qkv[which], preferred_element_type=jnp.float32)
        for head in range(heads):
            cols = slice(head * HD, (head + 1) * HD)
            part = raw[:, cols]
            if which < 2:
                part = part * rms_scale(part) * qk_gain[which : which + 1, cols]
            part = part.astype(jnp.bfloat16)
            if which == 0:
                q_out[head] = part
            else:
                kv_out[head, which - 1] = part


def front(sr, base, place, gain, w_qkv, qk_gain):
    rows, depth = sr.shape
    width = w_qkv.shape[2]
    heads = width // HD
    tile = 256
    share = depth // lax.axis_size("segment")
    return pl.pallas_call(
        functools.partial(front_kernel, heads),
        grid=(rows // tile,),
        in_specs=[
            pl.BlockSpec((tile, depth), lambda i: (i, 0)),
            pl.BlockSpec(base.shape, lambda i: (0, 0)),
            pl.BlockSpec((tile, 1), lambda i: (i, 0)),
            pl.BlockSpec((1, depth), lambda i: (0, 0)),
            pl.BlockSpec(w_qkv.shape, lambda i: (0, 0, 0)),
            pl.BlockSpec(qk_gain.shape, lambda i: (0, 0)),
        ],
        out_specs=[
            pl.BlockSpec((heads, tile, HD), lambda i: (0, i, 0)),
            pl.BlockSpec((heads, 2, tile, HD), lambda i: (0, 0, i, 0)),
            pl.BlockSpec((tile, share), lambda i: (i, 0)),
        ],
        out_shape=[
            jax.ShapeDtypeStruct((heads, rows, HD), jnp.bfloat16),
            jax.ShapeDtypeStruct((heads, 2, rows, HD), jnp.bfloat16),
            jax.ShapeDtypeStruct((rows, share), jnp.float32),
        ],
        scratch_shapes=[pltpu.VMEM((tile, depth), jnp.float32)],
        compiler_params=pltpu.CompilerParams(vmem_limit_bytes=48 * MIB),
        name="front",
    )(sr, base, place, gain, w_qkv, qk_gain)


def greet(targets):
    barrier = pltpu.get_barrier_semaphore()
    for target in targets:
        pl.semaphore_signal(barrier, inc=1, device_id=target, device_id_type=MESH)
    pl.semaphore_wait(barrier, len(targets))


def remote(src, dst, send, recv, target):
    return pltpu.make_async_remote_copy(
        src_ref=src, dst_ref=dst, send_sem=send, recv_sem=recv, device_id=target, device_id_type=MESH
    )


def middle_kernel(
    seqs, segs, groups, chunks, together,
    lists, counts, q, kv, w_out, share, out,
    kv_all, q_all, att, full, w_cols,
    kv_send, kv_recv, q_send, q_recv, fw_send, fw_recv, w_send, w_recv,
    z_send, z_recv, p_send, p_recv, own, own_chunk,
):
    me, seg = lax.axis_index("seq"), lax.axis_index("segment")
    rows = q.shape[1]
    part_rows = rows // groups
    size = part_rows // chunks
    half = size // 2
    head, part = me // groups, me % groups
    depth, cols = w_out.shape[0], w_out.shape[1] // segs
    window = lists.shape[0] // counts.shape[0]
    near_x, near_y, far = seg ^ 1, seg ^ 2, seg ^ 3
    greet([(seg, me ^ k) for k in range(1, seqs)] + [(seg ^ k, me) for k in range(1, segs)])

    blocks_source, blocks_part, blocks_chunk = rows // BLOCK, part_rows // BLOCK, size // BLOCK

    def blocks_of(which):
        return pl.ds(which * blocks_part, blocks_part)

    def chunk_rows(chunk):
        return pl.ds(pl.multiple_of(chunk * size, size), size)

    def landing(source, which):
        start = source * blocks_source + which * blocks_part
        return kv_all.at[:, pl.ds(start, blocks_part)]

    def kv_copy(target, source):
        return remote(
            kv.at[target // groups, :, blocks_of(target % groups)],
            landing(source, target % groups),
            kv_send.at[target],
            kv_recv.at[source],
            (seg, target),
        )

    def q_from(chunk, target):
        start = pl.multiple_of((target % groups) * part_rows + chunk * size, size)
        return q.at[target // groups, pl.ds(start, size), :]

    def q_copy(chunk, target, source):
        return remote(
            q_from(chunk, target),
            q_all.at[source, chunk_rows(chunk), :],
            q_send.at[chunk, target],
            q_recv.at[chunk, source],
            (seg, target),
        )

    def w_from(target):
        return w_out.at[:, pl.ds(pl.multiple_of(target * cols, cols), cols)]

    def w_to(source):
        return w_cols.at[pl.ds(pl.multiple_of(source * depth, depth), depth), :]

    def w_copy(target, source):
        return remote(
            w_from(target), w_to(source), w_send.at[target], w_recv.at[source], (target, me)
        )

    def forward(source, step, sender_part):
        slot = landing(source, sender_part)
        target = head * groups + lax.rem(part + step, groups)
        return remote(
            slot, slot, fw_send.at[source, step - 1], fw_recv.at[source, step - 1], (seg, target)
        )

    def spot(chunk, owner):
        lanes = pl.ds(pl.multiple_of((owner // groups) * HD, HD), HD)
        return full.at[seg, owner % groups, chunk_rows(chunk), lanes]

    def z_copy(chunk, target, owner):
        return remote(
            att.at[target, chunk_rows(chunk), :],
            spot(chunk, owner),
            z_send.at[chunk, target],
            z_recv.at[chunk, owner],
            (seg, target),
        )

    def own_copy(chunk):
        return pltpu.make_async_copy(
            att.at[me, chunk_rows(chunk), :], spot(chunk, me), own_chunk.at[chunk]
        )

    def pair_copy(chunk, kind, origin, to):
        at = pl.multiple_of(chunk * size + (half if kind == 3 else 0), half)
        piece = full.at[origin, :, pl.ds(at, size if kind < 2 else half), :]
        return remote(piece, piece, p_send.at[chunk, kind], p_recv.at[chunk, kind], (to, me))

    own_kv = pltpu.make_async_copy(kv.at[head, :, blocks_of(part)], landing(me, part), own.at[0])
    own_q = pltpu.make_async_copy(
        q.at[head, pl.ds(pl.multiple_of(part * part_rows, part_rows), part_rows), :], q_all.at[me], own.at[1]
    )
    own_w = pltpu.make_async_copy(w_from(seg), w_to(seg), own.at[2])
    own_kv.start()

    @pl.loop(1, seqs)
    def _(k):
        kv_copy(me ^ (seqs - k), me).start()

    own_q.start()
    own_w.start()

    @pl.loop(1, segs)
    def _(k):
        w_copy(seg ^ k, seg).start()

    own_kv.wait()
    for step in range(1, groups):
        forward(me, step, part).start()

    @pl.loop(1, seqs)
    def _(k):
        other = me ^ k
        kv_copy(me, other).wait_recv()
        for step in range(1, groups):
            forward(other, step, part).start()
        kv_copy(other, me).wait_send()

        @pl.loop(0, chunks)
        def _(chunk):
            q_copy(chunk, other, me).start()

    @pl.loop(0, seqs)
    def _(source):
        for step in range(1, groups):
            forward(source, step, lax.rem(part + groups - step, groups)).wait_recv()
            forward(source, step, part).wait_send()

    own_q.wait()

    column = lax.broadcasted_iota(jnp.int32, (BLOCK, window * BLOCK), 1)

    def one(source, local):
        block = source * blocks_source + part * blocks_part + local
        listed = [lists[block * window + w] for w in range(window)]
        keys = jnp.concatenate([kv_all[0, at] for at in listed], axis=0)
        values = jnp.concatenate([kv_all[1, at] for at in listed], axis=0)
        query = q_all[source, pl.ds(pl.multiple_of(local * BLOCK, BLOCK), BLOCK), :]
        scores = lax.dot_general(
            query, keys, (((1,), (1,)), ((), ())), preferred_element_type=jnp.float32
        ) * HD ** (-0.5)
        scores = jnp.where(column < counts[block] * BLOCK, scores, -jnp.inf)
        weights = jnp.exp(scores - jnp.max(scores, axis=1, keepdims=True))
        total = jnp.sum(weights, axis=1, keepdims=True)
        summed = jnp.dot(weights.astype(jnp.bfloat16), values, preferred_element_type=jnp.float32)
        return (summed / total).astype(jnp.bfloat16)

    def attend(chunk):
        @pl.loop(0, seqs * blocks_chunk // together)
        def _(step):
            places = []
            for i in range(together):
                index = step * together + i
                places.append((index // blocks_chunk, chunk * blocks_chunk + index % blocks_chunk))
            done = [one(*place) for place in places]
            for (source, local), value in zip(places, done):
                att[source, pl.ds(pl.multiple_of(local * BLOCK, BLOCK), BLOCK), :] = value

    @pl.loop(0, chunks + 3)
    def _(step):
        @pl.when(step < chunks)
        def _():
            @pl.loop(1, seqs)
            def _(k):
                q_copy(step, me, me ^ k).wait_recv()

            attend(step)

            @pl.loop(1, seqs)
            def _(k):
                z_copy(step, me ^ (seqs - k), me).start()

            own_copy(step).start()

        @pl.when(jnp.logical_and(step >= 1, step < chunks + 1))
        def _():
            chunk = step - 1
            own_copy(chunk).wait()

            @pl.loop(1, seqs)
            def _(k):
                z_copy(chunk, me, me ^ k).wait_recv()

            pair_copy(chunk, 0, seg, near_x).start()
            pair_copy(chunk, 1, seg, near_y).start()

        @pl.when(jnp.logical_and(step >= 2, step < chunks + 2))
        def _():
            chunk = step - 2
            pair_copy(chunk, 0, near_x, near_x).wait_recv()
            pair_copy(chunk, 2, near_x, near_y).start()
            pair_copy(chunk, 1, near_y, near_y).wait_recv()
            pair_copy(chunk, 3, near_y, near_x).start()

        @pl.when(step == 3)
        def _():
            own_w.wait()

            @pl.loop(1, segs)
            def _(k):
                w_copy(seg, seg ^ k).wait_recv()

        @pl.when(step >= 3)
        def _():
            chunk = step - 3
            pair_copy(chunk, 2, far, near_y).wait_recv()
            pair_copy(chunk, 3, far, near_x).wait_recv()
            here = chunk_rows(chunk)
            total = jnp.zeros((groups * size, cols), jnp.float32)
            for j in range(segs):
                piece = full[j, :, here, :].reshape(groups * size, depth)
                total += jnp.dot(
                    piece, w_cols[j * depth : (j + 1) * depth, :], preferred_element_type=jnp.float32
                )
            total = total.reshape(groups, size, cols)
            out[:, here, :] = (share[:, here, :] + total).astype(jnp.bfloat16)

    @pl.loop(0, chunks)
    def _(chunk):
        pair_copy(chunk, 0, seg, near_x).wait_send()
        pair_copy(chunk, 1, seg, near_y).wait_send()
        pair_copy(chunk, 2, near_x, near_y).wait_send()
        pair_copy(chunk, 3, near_y, near_x).wait_send()

        @pl.loop(1, seqs)
        def _(k):
            q_copy(chunk, me ^ k, me).wait_send()
            z_copy(chunk, me ^ k, me).wait_send()

    @pl.loop(1, segs)
    def _(k):
        w_copy(seg ^ k, seg).wait_send()


def middle(lists, counts, q, kv, w_out, share, seqs, segs, groups):
    heads, rows, _ = q.shape
    depth, width = w_out.shape
    part_rows = rows // groups
    chunks = min(CHUNKS, part_rows // BLOCK)
    cols = width // segs
    dma = pltpu.SemaphoreType.DMA
    anywhere = pl.BlockSpec(memory_space=pl.ANY)
    vmem = pl.BlockSpec(memory_space=pltpu.VMEM)
    smem = pl.BlockSpec(memory_space=pltpu.SMEM)
    return pl.pallas_call(
        functools.partial(middle_kernel, seqs, segs, groups, chunks, TOGETHER),
        in_specs=[smem, smem, anywhere, anywhere, anywhere, vmem],
        out_specs=vmem,
        out_shape=jax.ShapeDtypeStruct((groups, part_rows, cols), jnp.bfloat16),
        scratch_shapes=[
            pltpu.VMEM((2, seqs * rows // BLOCK, BLOCK, HD), jnp.bfloat16),
            pltpu.VMEM((seqs, part_rows, HD), jnp.bfloat16),
            pltpu.VMEM((seqs, part_rows, HD), jnp.bfloat16),
            pltpu.VMEM((segs, groups, part_rows, depth), jnp.bfloat16),
            pltpu.VMEM((segs * depth, cols), jnp.bfloat16),
            dma((seqs,)), dma((seqs,)), dma((chunks, seqs)), dma((chunks, seqs)),
            dma((seqs, max(groups - 1, 1))), dma((seqs, max(groups - 1, 1))),
            dma((segs,)), dma((segs,)),
            dma((chunks, seqs)), dma((chunks, seqs)), dma((chunks, 4)), dma((chunks, 4)),
            dma((3,)), dma((chunks,)),
        ],
        compiler_params=pltpu.CompilerParams(
            collective_id=0, has_side_effects=True, vmem_limit_bytes=48 * MIB
        ),
        name="middle",
    )(lists, counts, q, kv.reshape(heads, 2, rows // BLOCK, BLOCK, HD), w_out, share)


def on_device(
    sr_tokens, base_latent, upsample_map, norm_gain, w_qkv, qk_gain, w_out, block_lists, block_counts
):
    seqs, segs = lax.axis_size("seq"), lax.axis_size("segment")
    rank = lax.axis_index("seq")
    rows = sr_tokens.shape[0]
    heads = w_qkv.shape[2] // HD
    groups = seqs // heads
    part_rows = rows // groups
    padded = padded_2(base_latent, "seq", BASE_FT)
    place = (upsample_map - (rank * base_latent.shape[0] - BASE_FT))[:, None]
    q, kv, share = front(sr_tokens, padded, place, norm_gain[None], w_qkv, qk_gain)
    out = middle(
        block_lists.reshape(-1), block_counts, q, kv, w_out,
        share.reshape(groups, part_rows, -1), seqs, segs, groups,
    )
    return out.reshape(rows, -1)


def solution(mesh):
    placed = (
        P("seq", None),
        P("seq", None),
        P("seq"),
        P(),
        P(None, None, "segment"),
        P(None, "segment"),
        P("segment", None),
        P(),
        P(),
    )
    return jax.shard_map(
        on_device, mesh=mesh, in_specs=placed, out_specs=P("seq", "segment"), check_vma=False
    )
```

```python
import functools

import jax
import jax.numpy as jnp
from jax import lax
from jax.experimental import pallas as pl
from jax.experimental.pallas import tpu as pltpu
from jax.sharding import PartitionSpec as P

HD = 128
BASE_FT = 64
BLOCK = 64
EPSILON = 1e-06
CHUNKS = 8
TOGETHER = 4
MESH = pl.DeviceIdType.MESH
MIB = 2**20


def padded_2(x, axis, width):
    count, length = lax.axis_size(axis), x.shape[0]
    up = [(i, (i + 1) % count) for i in range(count - 1)]
    down = [(j, i) for i, j in up]
    before = lax.ppermute(lax.slice_in_dim(x, length - width, length, axis=0), axis, up)
    after = lax.ppermute(lax.slice_in_dim(x, 0, width, axis=0), axis, down)
    return jnp.concatenate([before, x, after], axis=0)


def rms_scale(tensor):
    return lax.rsqrt(jnp.mean(tensor * tensor, axis=-1, keepdims=True) + EPSILON)


def front_kernel(heads, sr, base, place, gain, w_qkv, qk_gain, normed_out, kv_out, share_out, mixed):
    rows = sr.shape[0]
    count = base.shape[0]
    hot = (lax.broadcasted_iota(jnp.int32, (rows, count), 1) == place[...]).astype(jnp.bfloat16)
    condition = jnp.dot(hot, base[...], preferred_element_type=jnp.float32)
    mixed[...] = sr[...].astype(jnp.float32) + condition
    width = share_out.shape[1]
    start = pl.multiple_of(lax.axis_index("segment") * width, width)
    share_out[...] = mixed[:, pl.ds(start, width)]
    whole = mixed[...]
    normed = (whole * rms_scale(whole) * gain[...]).astype(jnp.bfloat16)
    normed_out[...] = normed
    for which in range(2):
        raw = jnp.dot(normed, w_qkv[which], preferred_element_type=jnp.float32)
        for head in range(heads):
            cols = slice(head * HD, (head + 1) * HD)
            part = raw[:, cols]
            if which == 0:
                part = part * rms_scale(part) * qk_gain[1:2, cols]
            kv_out[head, which] = part.astype(jnp.bfloat16)


def front(sr, base, place, gain, w_qkv, qk_gain):
    rows, depth = sr.shape
    width = w_qkv.shape[2]
    heads = width // HD
    tile = 256
    share = depth // lax.axis_size("segment")
    return pl.pallas_call(
        functools.partial(front_kernel, heads),
        grid=(rows // tile,),
        in_specs=[
            pl.BlockSpec((tile, depth), lambda i: (i, 0)),
            pl.BlockSpec(base.shape, lambda i: (0, 0)),
            pl.BlockSpec((tile, 1), lambda i: (i, 0)),
            pl.BlockSpec((1, depth), lambda i: (0, 0)),
            pl.BlockSpec((pl.Element(2), pl.Element(depth), pl.Element(width)), lambda i: (1, 0, 0)),
            pl.BlockSpec(qk_gain.shape, lambda i: (0, 0)),
        ],
        out_specs=[
            pl.BlockSpec((tile, depth), lambda i: (i, 0)),
            pl.BlockSpec((heads, 2, tile, HD), lambda i: (0, 0, i, 0)),
            pl.BlockSpec((tile, share), lambda i: (i, 0)),
        ],
        out_shape=[
            jax.ShapeDtypeStruct((rows, depth), jnp.bfloat16),
            jax.ShapeDtypeStruct((heads, 2, rows, HD), jnp.bfloat16),
            jax.ShapeDtypeStruct((rows, share), jnp.float32),
        ],
        scratch_shapes=[pltpu.VMEM((tile, depth), jnp.float32)],
        compiler_params=pltpu.CompilerParams(vmem_limit_bytes=48 * MIB),
        name="front",
    )(sr, base, place, gain, w_qkv, qk_gain)


def greet(targets):
    barrier = pltpu.get_barrier_semaphore()
    for target in targets:
        pl.semaphore_signal(barrier, inc=1, device_id=target, device_id_type=MESH)
    pl.semaphore_wait(barrier, len(targets))


def remote(src, dst, send, recv, target):
    return pltpu.make_async_remote_copy(
        src_ref=src, dst_ref=dst, send_sem=send, recv_sem=recv, device_id=target, device_id_type=MESH
    )


def middle_kernel(
    seqs, segs, groups, chunks, together,
    lists, counts, normed, w_qkv, qk_gain, kv, w_out, share, out,
    q, rows_in, w_q, kv_all, q_all, att, full, w_cols,
    kv_send, kv_recv, q_send, q_recv, fw_send, fw_recv, w_send, w_recv,
    z_send, z_recv, p_send, p_recv, own, own_chunk,
):
    me, seg = lax.axis_index("seq"), lax.axis_index("segment")
    rows = q.shape[1]
    load_rows = pltpu.make_async_copy(normed, rows_in, own.at[3])
    load_w = pltpu.make_async_copy(w_qkv.at[0], w_q, own.at[4])
    load_rows.start()
    load_w.start()
    part_rows = rows // groups
    size = part_rows // chunks
    half = size // 2
    head, part = me // groups, me % groups
    depth, cols = w_out.shape[0], w_out.shape[1] // segs
    window = lists.shape[0] // counts.shape[0]
    near_x, near_y, far = seg ^ 1, seg ^ 2, seg ^ 3
    greet([(seg, me ^ k) for k in range(1, seqs)] + [(seg ^ k, me) for k in range(1, segs)])

    blocks_source, blocks_part, blocks_chunk = rows // BLOCK, part_rows // BLOCK, size // BLOCK

    def blocks_of(which):
        return pl.ds(which * blocks_part, blocks_part)

    def chunk_rows(chunk):
        return pl.ds(pl.multiple_of(chunk * size, size), size)

    def landing(source, which):
        start = source * blocks_source + which * blocks_part
        return kv_all.at[:, pl.ds(start, blocks_part)]

    def kv_copy(target, source):
        return remote(
            kv.at[target // groups, :, blocks_of(target % groups)],
            landing(source, target % groups),
            kv_send.at[target],
            kv_recv.at[source],
            (seg, target),
        )

    def q_from(chunk, target):
        start = pl.multiple_of((target % groups) * part_rows + chunk * size, size)
        return q.at[target // groups, pl.ds(start, size), :]

    def q_copy(chunk, target, source):
        return remote(
            q_from(chunk, target),
            q_all.at[source, chunk_rows(chunk), :],
            q_send.at[chunk, target],
            q_recv.at[chunk, source],
            (seg, target),
        )

    def w_from(target):
        return w_out.at[:, pl.ds(pl.multiple_of(target * cols, cols), cols)]

    def w_to(source):
        return w_cols.at[pl.ds(pl.multiple_of(source * depth, depth), depth), :]

    def w_copy(target, source):
        return remote(
            w_from(target), w_to(source), w_send.at[target], w_recv.at[source], (target, me)
        )

    def forward(source, step, sender_part):
        slot = landing(source, sender_part)
        target = head * groups + lax.rem(part + step, groups)
        return remote(
            slot, slot, fw_send.at[source, step - 1], fw_recv.at[source, step - 1], (seg, target)
        )

    def spot(chunk, owner):
        lanes = pl.ds(pl.multiple_of((owner // groups) * HD, HD), HD)
        return full.at[seg, owner % groups, chunk_rows(chunk), lanes]

    def z_copy(chunk, target, owner):
        return remote(
            att.at[target, chunk_rows(chunk), :],
            spot(chunk, owner),
            z_send.at[chunk, target],
            z_recv.at[chunk, owner],
            (seg, target),
        )

    def own_copy(chunk):
        return pltpu.make_async_copy(
            att.at[me, chunk_rows(chunk), :], spot(chunk, me), own_chunk.at[chunk]
        )

    def pair_copy(chunk, kind, origin, to):
        at = pl.multiple_of(chunk * size + (half if kind == 3 else 0), half)
        piece = full.at[origin, :, pl.ds(at, size if kind < 2 else half), :]
        return remote(piece, piece, p_send.at[chunk, kind], p_recv.at[chunk, kind], (to, me))

    own_kv = pltpu.make_async_copy(kv.at[head, :, blocks_of(part)], landing(me, part), own.at[0])
    own_q = pltpu.make_async_copy(
        q.at[head, pl.ds(pl.multiple_of(part * part_rows, part_rows), part_rows), :], q_all.at[me], own.at[1]
    )
    own_w = pltpu.make_async_copy(w_from(seg), w_to(seg), own.at[2])
    own_kv.start()

    @pl.loop(1, seqs)
    def _(k):
        kv_copy(me ^ (seqs - k), me).start()

    own_w.start()

    @pl.loop(1, segs)
    def _(k):
        w_copy(seg ^ k, seg).start()

    own_kv.wait()
    for step in range(1, groups):
        forward(me, step, part).start()

    load_rows.wait()
    load_w.wait()
    tile = 256

    @pl.loop(0, rows // tile)
    def _(i):
        here = pl.ds(pl.multiple_of(i * tile, tile), tile)
        raw = jnp.dot(rows_in[here, :], w_q[...], preferred_element_type=jnp.float32)
        for h in range(q.shape[0]):
            lanes = slice(h * HD, (h + 1) * HD)
            piece = raw[:, lanes]
            piece = piece * rms_scale(piece) * qk_gain[0:1, lanes]
            q[h, here, :] = piece.astype(jnp.bfloat16)

    own_q.start()

    @pl.loop(1, seqs)
    def _(k):
        other = me ^ k
        kv_copy(me, other).wait_recv()
        for step in range(1, groups):
            forward(other, step, part).start()
        kv_copy(other, me).wait_send()
        q_copy(0, other, me).start()

    @pl.loop(1, chunks)
    def _(chunk):
        @pl.loop(1, seqs)
        def _(k):
            q_copy(chunk, me ^ (seqs - k), me).start()

    @pl.loop(0, seqs)
    def _(source):
        for step in range(1, groups):
            forward(source, step, lax.rem(part + groups - step, groups)).wait_recv()
            forward(source, step, part).wait_send()

    own_q.wait()

    column = lax.broadcasted_iota(jnp.int32, (BLOCK, window * BLOCK), 1)

    def one(source, local):
        block = source * blocks_source + part * blocks_part + local
        listed = [lists[block * window + w] for w in range(window)]
        keys = jnp.concatenate([kv_all[0, at] for at in listed], axis=0)
        values = jnp.concatenate([kv_all[1, at] for at in listed], axis=0)
        query = q_all[source, pl.ds(pl.multiple_of(local * BLOCK, BLOCK), BLOCK), :]
        scores = lax.dot_general(
            query, keys, (((1,), (1,)), ((), ())), preferred_element_type=jnp.float32
        ) * HD ** (-0.5)
        scores = jnp.where(column < counts[block] * BLOCK, scores, -jnp.inf)
        weights = jnp.exp(scores - jnp.max(scores, axis=1, keepdims=True))
        total = jnp.sum(weights, axis=1, keepdims=True)
        summed = jnp.dot(weights.astype(jnp.bfloat16), values, preferred_element_type=jnp.float32)
        return (summed / total).astype(jnp.bfloat16)

    def attend(chunk):
        @pl.loop(0, seqs * blocks_chunk // together)
        def _(step):
            places = []
            for i in range(together):
                index = step * together + i
                places.append((index // blocks_chunk, chunk * blocks_chunk + index % blocks_chunk))
            done = [one(*place) for place in places]
            for (source, local), value in zip(places, done):
                att[source, pl.ds(pl.multiple_of(local * BLOCK, BLOCK), BLOCK), :] = value

    @pl.loop(0, chunks + 3)
    def _(step):
        @pl.when(step < chunks)
        def _():
            @pl.loop(1, seqs)
            def _(k):
                q_copy(step, me, me ^ k).wait_recv()

            attend(step)

            @pl.loop(1, seqs)
            def _(k):
                z_copy(step, me ^ (seqs - k), me).start()

            own_copy(step).start()

        @pl.when(jnp.logical_and(step >= 1, step < chunks + 1))
        def _():
            chunk = step - 1
            own_copy(chunk).wait()

            @pl.loop(1, seqs)
            def _(k):
                z_copy(chunk, me, me ^ k).wait_recv()

            pair_copy(chunk, 0, seg, near_x).start()
            pair_copy(chunk, 1, seg, near_y).start()

        @pl.when(jnp.logical_and(step >= 2, step < chunks + 2))
        def _():
            chunk = step - 2
            pair_copy(chunk, 0, near_x, near_x).wait_recv()
            pair_copy(chunk, 2, near_x, near_y).start()
            pair_copy(chunk, 1, near_y, near_y).wait_recv()
            pair_copy(chunk, 3, near_y, near_x).start()

        @pl.when(step == 3)
        def _():
            own_w.wait()

            @pl.loop(1, segs)
            def _(k):
                w_copy(seg, seg ^ k).wait_recv()

        @pl.when(step >= 3)
        def _():
            chunk = step - 3
            pair_copy(chunk, 2, far, near_y).wait_recv()
            pair_copy(chunk, 3, far, near_x).wait_recv()
            here = chunk_rows(chunk)
            total = jnp.zeros((groups * size, cols), jnp.float32)
            for j in range(segs):
                piece = full[j, :, here, :].reshape(groups * size, depth)
                total += jnp.dot(
                    piece, w_cols[j * depth : (j + 1) * depth, :], preferred_element_type=jnp.float32
                )
            total = total.reshape(groups, size, cols)
            out[:, here, :] = (share[:, here, :] + total).astype(jnp.bfloat16)

    @pl.loop(0, chunks)
    def _(chunk):
        pair_copy(chunk, 0, seg, near_x).wait_send()
        pair_copy(chunk, 1, seg, near_y).wait_send()
        pair_copy(chunk, 2, near_x, near_y).wait_send()
        pair_copy(chunk, 3, near_y, near_x).wait_send()

        @pl.loop(1, seqs)
        def _(k):
            q_copy(chunk, me ^ k, me).wait_send()
            z_copy(chunk, me ^ k, me).wait_send()

    @pl.loop(1, segs)
    def _(k):
        w_copy(seg ^ k, seg).wait_send()


def middle(lists, counts, normed, w_qkv, qk_gain, kv, w_out, share, seqs, segs, groups):
    heads, _, rows, _ = kv.shape
    depth, width = w_out.shape
    part_rows = rows // groups
    chunks = min(CHUNKS, part_rows // BLOCK)
    cols = width // segs
    dma = pltpu.SemaphoreType.DMA
    anywhere = pl.BlockSpec(memory_space=pl.ANY)
    vmem = pl.BlockSpec(memory_space=pltpu.VMEM)
    smem = pl.BlockSpec(memory_space=pltpu.SMEM)
    return pl.pallas_call(
        functools.partial(middle_kernel, seqs, segs, groups, chunks, TOGETHER),
        in_specs=[smem, smem, anywhere, anywhere, vmem, anywhere, anywhere, vmem],
        out_specs=vmem,
        out_shape=jax.ShapeDtypeStruct((groups, part_rows, cols), jnp.bfloat16),
        scratch_shapes=[
            pltpu.VMEM((heads, rows, HD), jnp.bfloat16),
            pltpu.VMEM(normed.shape, jnp.bfloat16),
            pltpu.VMEM(w_qkv.shape[1:], jnp.bfloat16),
            pltpu.VMEM((2, seqs * rows // BLOCK, BLOCK, HD), jnp.bfloat16),
            pltpu.VMEM((seqs, part_rows, HD), jnp.bfloat16),
            pltpu.VMEM((seqs, part_rows, HD), jnp.bfloat16),
            pltpu.VMEM((segs, groups, part_rows, depth), jnp.bfloat16),
            pltpu.VMEM((segs * depth, cols), jnp.bfloat16),
            dma((seqs,)), dma((seqs,)), dma((chunks, seqs)), dma((chunks, seqs)),
            dma((seqs, max(groups - 1, 1))), dma((seqs, max(groups - 1, 1))),
            dma((segs,)), dma((segs,)),
            dma((chunks, seqs)), dma((chunks, seqs)), dma((chunks, 4)), dma((chunks, 4)),
            dma((5,)), dma((chunks,)),
        ],
        compiler_params=pltpu.CompilerParams(
            collective_id=0, has_side_effects=True, vmem_limit_bytes=48 * MIB
        ),
        name="middle",
    )(
        lists, counts, normed, w_qkv, qk_gain,
        kv.reshape(heads, 2, rows // BLOCK, BLOCK, HD), w_out, share,
    )


def on_device(
    sr_tokens, base_latent, upsample_map, norm_gain, w_qkv, qk_gain, w_out, block_lists, block_counts
):
    seqs, segs = lax.axis_size("seq"), lax.axis_size("segment")
    rank = lax.axis_index("seq")
    rows = sr_tokens.shape[0]
    heads = w_qkv.shape[2] // HD
    groups = seqs // heads
    part_rows = rows // groups
    padded = padded_2(base_latent, "seq", BASE_FT)
    place = (upsample_map - (rank * base_latent.shape[0] - BASE_FT))[:, None]
    normed, kv, share = front(sr_tokens, padded, place, norm_gain[None], w_qkv, qk_gain)
    out = middle(
        block_lists.reshape(-1), block_counts, normed, w_qkv, qk_gain, kv, w_out,
        share.reshape(groups, part_rows, -1), seqs, segs, groups,
    )
    return out.reshape(rows, -1)


def solution(mesh):
    placed = (
        P("seq", None),
        P("seq", None),
        P("seq"),
        P(),
        P(None, None, "segment"),
        P(None, "segment"),
        P("segment", None),
        P(),
        P(),
    )
    return jax.shard_map(
        on_device, mesh=mesh, in_specs=placed, out_specs=P("seq", "segment"), check_vma=False
    )
```

```python
import functools

import jax
import jax.numpy as jnp
from jax import lax
from jax.experimental import pallas as pl
from jax.experimental.pallas import tpu as pltpu
from jax.sharding import PartitionSpec as P

HD = 128
BASE_FT = 64
BLOCK = 64
EPSILON = 1e-06
CHUNKS = 8
TOGETHER = 8
MESH = pl.DeviceIdType.MESH
MIB = 2**20


def padded_2(x, axis, width):
    count, length = lax.axis_size(axis), x.shape[0]
    up = [(i, (i + 1) % count) for i in range(count - 1)]
    down = [(j, i) for i, j in up]
    before = lax.ppermute(lax.slice_in_dim(x, length - width, length, axis=0), axis, up)
    after = lax.ppermute(lax.slice_in_dim(x, 0, width, axis=0), axis, down)
    return jnp.concatenate([before, x, after], axis=0)


def rms_scale(tensor):
    return lax.rsqrt(jnp.mean(tensor * tensor, axis=-1, keepdims=True) + EPSILON)


def front_kernel(heads, sr, base, place, gain, w_qkv, qk_gain, normed_out, kv_out, share_out, mixed):
    rows = sr.shape[0]
    count = base.shape[0]
    hot = (lax.broadcasted_iota(jnp.int32, (rows, count), 1) == place[...]).astype(jnp.bfloat16)
    condition = jnp.dot(hot, base[...], preferred_element_type=jnp.float32)
    mixed[...] = sr[...].astype(jnp.float32) + condition
    width = share_out.shape[1]
    start = pl.multiple_of(lax.axis_index("segment") * width, width)
    share_out[...] = mixed[:, pl.ds(start, width)]
    whole = mixed[...]
    normed = (whole * rms_scale(whole) * gain[...]).astype(jnp.bfloat16)
    normed_out[...] = normed
    for which in range(2):
        raw = jnp.dot(normed, w_qkv[which], preferred_element_type=jnp.float32)
        for head in range(heads):
            cols = slice(head * HD, (head + 1) * HD)
            part = raw[:, cols]
            if which == 0:
                part = part * rms_scale(part) * qk_gain[1:2, cols]
            kv_out[head, which] = part.astype(jnp.bfloat16)


def front(sr, base, place, gain, w_qkv, qk_gain):
    rows, depth = sr.shape
    width = w_qkv.shape[2]
    heads = width // HD
    tile = 256
    share = depth // lax.axis_size("segment")
    return pl.pallas_call(
        functools.partial(front_kernel, heads),
        grid=(rows // tile,),
        in_specs=[
            pl.BlockSpec((tile, depth), lambda i: (i, 0)),
            pl.BlockSpec(base.shape, lambda i: (0, 0)),
            pl.BlockSpec((tile, 1), lambda i: (i, 0)),
            pl.BlockSpec((1, depth), lambda i: (0, 0)),
            pl.BlockSpec((pl.Element(2), pl.Element(depth), pl.Element(width)), lambda i: (1, 0, 0)),
            pl.BlockSpec(qk_gain.shape, lambda i: (0, 0)),
        ],
        out_specs=[
            pl.BlockSpec((tile, depth), lambda i: (i, 0)),
            pl.BlockSpec((heads, 2, tile, HD), lambda i: (0, 0, i, 0)),
            pl.BlockSpec((tile, share), lambda i: (i, 0)),
        ],
        out_shape=[
            jax.ShapeDtypeStruct((rows, depth), jnp.bfloat16),
            jax.ShapeDtypeStruct((heads, 2, rows, HD), jnp.bfloat16),
            jax.ShapeDtypeStruct((rows, share), jnp.float32),
        ],
        scratch_shapes=[pltpu.VMEM((tile, depth), jnp.float32)],
        compiler_params=pltpu.CompilerParams(vmem_limit_bytes=48 * MIB),
        name="front",
    )(sr, base, place, gain, w_qkv, qk_gain)


def greet(targets):
    barrier = pltpu.get_barrier_semaphore()
    for target in targets:
        pl.semaphore_signal(barrier, inc=1, device_id=target, device_id_type=MESH)
    pl.semaphore_wait(barrier, len(targets))


def remote(src, dst, send, recv, target):
    return pltpu.make_async_remote_copy(
        src_ref=src, dst_ref=dst, send_sem=send, recv_sem=recv, device_id=target, device_id_type=MESH
    )


def middle_kernel(
    seqs, segs, groups, chunks, together,
    lists, counts, normed, w_qkv, qk_gain, kv, w_out, share, out,
    q, rows_in, w_q, kv_all, q_all, att, full, w_cols,
    kv_send, kv_recv, q_send, q_recv, fw_send, fw_recv, w_send, w_recv,
    z_send, z_recv, p_send, p_recv, own, own_chunk,
):
    me, seg = lax.axis_index("seq"), lax.axis_index("segment")
    rows = q.shape[1]
    load_rows = pltpu.make_async_copy(normed, rows_in, own.at[3])
    load_w = pltpu.make_async_copy(w_qkv.at[0], w_q, own.at[4])
    load_rows.start()
    load_w.start()
    part_rows = rows // groups
    size = part_rows // chunks
    half = size // 2
    head, part = me // groups, me % groups
    depth, cols = w_out.shape[0], w_out.shape[1] // segs
    window = lists.shape[0] // counts.shape[0]
    near_x, near_y, far = seg ^ 1, seg ^ 2, seg ^ 3
    greet([(seg, me ^ k) for k in range(1, seqs)] + [(seg ^ k, me) for k in range(1, segs)])

    blocks_source, blocks_part, blocks_chunk = rows // BLOCK, part_rows // BLOCK, size // BLOCK

    def blocks_of(which):
        return pl.ds(which * blocks_part, blocks_part)

    def chunk_rows(chunk):
        return pl.ds(pl.multiple_of(chunk * size, size), size)

    def landing(source, which):
        start = source * blocks_source + which * blocks_part
        return kv_all.at[:, pl.ds(start, blocks_part)]

    def kv_copy(target, source):
        return remote(
            kv.at[target // groups, :, blocks_of(target % groups)],
            landing(source, target % groups),
            kv_send.at[target],
            kv_recv.at[source],
            (seg, target),
        )

    def q_from(chunk, target):
        start = pl.multiple_of((target % groups) * part_rows + chunk * size, size)
        return q.at[target // groups, pl.ds(start, size), :]

    def q_copy(chunk, target, source):
        return remote(
            q_from(chunk, target),
            q_all.at[source, chunk_rows(chunk), :],
            q_send.at[chunk, target],
            q_recv.at[chunk, source],
            (seg, target),
        )

    def w_from(target):
        return w_out.at[:, pl.ds(pl.multiple_of(target * cols, cols), cols)]

    def w_to(source):
        return w_cols.at[pl.ds(pl.multiple_of(source * depth, depth), depth), :]

    def w_copy(target, source):
        return remote(
            w_from(target), w_to(source), w_send.at[target], w_recv.at[source], (target, me)
        )

    def forward(source, step, sender_part):
        slot = landing(source, sender_part)
        target = head * groups + lax.rem(part + step, groups)
        return remote(
            slot, slot, fw_send.at[source, step - 1], fw_recv.at[source, step - 1], (seg, target)
        )

    def spot(chunk, owner):
        lanes = pl.ds(pl.multiple_of((owner // groups) * HD, HD), HD)
        return full.at[seg, owner % groups, chunk_rows(chunk), lanes]

    def z_copy(chunk, target, owner):
        return remote(
            att.at[target, chunk_rows(chunk), :],
            spot(chunk, owner),
            z_send.at[chunk, target],
            z_recv.at[chunk, owner],
            (seg, target),
        )

    def own_copy(chunk):
        return pltpu.make_async_copy(
            att.at[me, chunk_rows(chunk), :], spot(chunk, me), own_chunk.at[chunk]
        )

    def pair_copy(chunk, kind, origin, to):
        at = pl.multiple_of(chunk * size + (half if kind == 3 else 0), half)
        piece = full.at[origin, :, pl.ds(at, size if kind < 2 else half), :]
        return remote(piece, piece, p_send.at[chunk, kind], p_recv.at[chunk, kind], (to, me))

    own_kv = pltpu.make_async_copy(kv.at[head, :, blocks_of(part)], landing(me, part), own.at[0])
    own_q = pltpu.make_async_copy(
        q.at[head, pl.ds(pl.multiple_of(part * part_rows, part_rows), part_rows), :], q_all.at[me], own.at[1]
    )
    own_w = pltpu.make_async_copy(w_from(seg), w_to(seg), own.at[2])
    own_kv.start()

    @pl.loop(1, seqs)
    def _(k):
        kv_copy(me ^ (seqs - k), me).start()

    own_w.start()

    @pl.loop(1, segs)
    def _(k):
        w_copy(seg ^ k, seg).start()

    own_kv.wait()
    for step in range(1, groups):
        forward(me, step, part).start()

    load_rows.wait()
    load_w.wait()
    tile = 256

    @pl.loop(0, rows // tile)
    def _(i):
        here = pl.ds(pl.multiple_of(i * tile, tile), tile)
        raw = jnp.dot(rows_in[here, :], w_q[...], preferred_element_type=jnp.float32)
        for h in range(q.shape[0]):
            lanes = slice(h * HD, (h + 1) * HD)
            piece = raw[:, lanes]
            piece = piece * rms_scale(piece) * qk_gain[0:1, lanes]
            q[h, here, :] = piece.astype(jnp.bfloat16)

    own_q.start()

    @pl.loop(1, seqs)
    def _(k):
        other = me ^ k
        kv_copy(me, other).wait_recv()
        for step in range(1, groups):
            forward(other, step, part).start()
        kv_copy(other, me).wait_send()
        q_copy(0, other, me).start()

    @pl.loop(1, chunks)
    def _(chunk):
        @pl.loop(1, seqs)
        def _(k):
            q_copy(chunk, me ^ (seqs - k), me).start()

    @pl.loop(0, seqs)
    def _(source):
        for step in range(1, groups):
            forward(source, step, lax.rem(part + groups - step, groups)).wait_recv()
            forward(source, step, part).wait_send()

    own_q.wait()

    column = lax.broadcasted_iota(jnp.int32, (BLOCK, window * BLOCK), 1)

    def one(source, local):
        block = source * blocks_source + part * blocks_part + local
        listed = [lists[block * window + w] for w in range(window)]
        keys = jnp.concatenate([kv_all[0, at] for at in listed], axis=0)
        values = jnp.concatenate([kv_all[1, at] for at in listed], axis=0)
        query = q_all[source, pl.ds(pl.multiple_of(local * BLOCK, BLOCK), BLOCK), :]
        scores = lax.dot_general(
            query, keys, (((1,), (1,)), ((), ())), preferred_element_type=jnp.float32
        ) * HD ** (-0.5)
        scores = jnp.where(column < counts[block] * BLOCK, scores, -jnp.inf)
        weights = jnp.exp(scores - jnp.max(scores, axis=1, keepdims=True))
        total = jnp.sum(weights, axis=1, keepdims=True)
        summed = jnp.dot(weights.astype(jnp.bfloat16), values, preferred_element_type=jnp.float32)
        return (summed / total).astype(jnp.bfloat16)

    def attend(chunk):
        @pl.loop(0, seqs * blocks_chunk // together)
        def _(step):
            places = []
            for i in range(together):
                index = step * together + i
                places.append((index // blocks_chunk, chunk * blocks_chunk + index % blocks_chunk))
            done = [one(*place) for place in places]
            for (source, local), value in zip(places, done):
                att[source, pl.ds(pl.multiple_of(local * BLOCK, BLOCK), BLOCK), :] = value

    @pl.loop(0, chunks + 3)
    def _(step):
        @pl.when(step < chunks)
        def _():
            @pl.loop(1, seqs)
            def _(k):
                q_copy(step, me, me ^ k).wait_recv()

            attend(step)

            @pl.loop(1, seqs)
            def _(k):
                z_copy(step, me ^ (seqs - k), me).start()

            own_copy(step).start()

        @pl.when(jnp.logical_and(step >= 1, step < chunks + 1))
        def _():
            chunk = step - 1
            own_copy(chunk).wait()

            @pl.loop(1, seqs)
            def _(k):
                z_copy(chunk, me, me ^ k).wait_recv()

            pair_copy(chunk, 0, seg, near_x).start()
            pair_copy(chunk, 1, seg, near_y).start()

        @pl.when(jnp.logical_and(step >= 2, step < chunks + 2))
        def _():
            chunk = step - 2
            pair_copy(chunk, 0, near_x, near_x).wait_recv()
            pair_copy(chunk, 2, near_x, near_y).start()
            pair_copy(chunk, 1, near_y, near_y).wait_recv()
            pair_copy(chunk, 3, near_y, near_x).start()

        @pl.when(step == 3)
        def _():
            own_w.wait()

            @pl.loop(1, segs)
            def _(k):
                w_copy(seg, seg ^ k).wait_recv()

        @pl.when(step >= 3)
        def _():
            chunk = step - 3
            pair_copy(chunk, 2, far, near_y).wait_recv()
            pair_copy(chunk, 3, far, near_x).wait_recv()
            here = chunk_rows(chunk)
            total = jnp.zeros((groups * size, cols), jnp.float32)
            for j in range(segs):
                piece = full[j, :, here, :].reshape(groups * size, depth)
                total += jnp.dot(
                    piece, w_cols[j * depth : (j + 1) * depth, :], preferred_element_type=jnp.float32
                )
            total = total.reshape(groups, size, cols)
            out[:, here, :] = (share[:, here, :] + total).astype(jnp.bfloat16)

    @pl.loop(0, chunks)
    def _(chunk):
        pair_copy(chunk, 0, seg, near_x).wait_send()
        pair_copy(chunk, 1, seg, near_y).wait_send()
        pair_copy(chunk, 2, near_x, near_y).wait_send()
        pair_copy(chunk, 3, near_y, near_x).wait_send()

        @pl.loop(1, seqs)
        def _(k):
            q_copy(chunk, me ^ k, me).wait_send()
            z_copy(chunk, me ^ k, me).wait_send()

    @pl.loop(1, segs)
    def _(k):
        w_copy(seg ^ k, seg).wait_send()


def middle(lists, counts, normed, w_qkv, qk_gain, kv, w_out, share, seqs, segs, groups):
    heads, _, rows, _ = kv.shape
    depth, width = w_out.shape
    part_rows = rows // groups
    chunks = min(CHUNKS, part_rows // BLOCK)
    cols = width // segs
    dma = pltpu.SemaphoreType.DMA
    anywhere = pl.BlockSpec(memory_space=pl.ANY)
    vmem = pl.BlockSpec(memory_space=pltpu.VMEM)
    smem = pl.BlockSpec(memory_space=pltpu.SMEM)
    return pl.pallas_call(
        functools.partial(middle_kernel, seqs, segs, groups, chunks, TOGETHER),
        in_specs=[smem, smem, anywhere, anywhere, vmem, anywhere, anywhere, vmem],
        out_specs=vmem,
        out_shape=jax.ShapeDtypeStruct((groups, part_rows, cols), jnp.bfloat16),
        scratch_shapes=[
            pltpu.VMEM((heads, rows, HD), jnp.bfloat16),
            pltpu.VMEM(normed.shape, jnp.bfloat16),
            pltpu.VMEM(w_qkv.shape[1:], jnp.bfloat16),
            pltpu.VMEM((2, seqs * rows // BLOCK, BLOCK, HD), jnp.bfloat16),
            pltpu.VMEM((seqs, part_rows, HD), jnp.bfloat16),
            pltpu.VMEM((seqs, part_rows, HD), jnp.bfloat16),
            pltpu.VMEM((segs, groups, part_rows, depth), jnp.bfloat16),
            pltpu.VMEM((segs * depth, cols), jnp.bfloat16),
            dma((seqs,)), dma((seqs,)), dma((chunks, seqs)), dma((chunks, seqs)),
            dma((seqs, max(groups - 1, 1))), dma((seqs, max(groups - 1, 1))),
            dma((segs,)), dma((segs,)),
            dma((chunks, seqs)), dma((chunks, seqs)), dma((chunks, 4)), dma((chunks, 4)),
            dma((5,)), dma((chunks,)),
        ],
        compiler_params=pltpu.CompilerParams(
            collective_id=0, has_side_effects=True, vmem_limit_bytes=48 * MIB
        ),
        name="middle",
    )(
        lists, counts, normed, w_qkv, qk_gain,
        kv.reshape(heads, 2, rows // BLOCK, BLOCK, HD), w_out, share,
    )


def on_device(
    sr_tokens, base_latent, upsample_map, norm_gain, w_qkv, qk_gain, w_out, block_lists, block_counts
):
    seqs, segs = lax.axis_size("seq"), lax.axis_size("segment")
    rank = lax.axis_index("seq")
    rows = sr_tokens.shape[0]
    heads = w_qkv.shape[2] // HD
    groups = seqs // heads
    part_rows = rows // groups
    padded = padded_2(base_latent, "seq", BASE_FT)
    place = (upsample_map - (rank * base_latent.shape[0] - BASE_FT))[:, None]
    normed, kv, share = front(sr_tokens, padded, place, norm_gain[None], w_qkv, qk_gain)
    out = middle(
        block_lists.reshape(-1), block_counts, normed, w_qkv, qk_gain, kv, w_out,
        share.reshape(groups, part_rows, -1), seqs, segs, groups,
    )
    return out.reshape(rows, -1)


def solution(mesh):
    placed = (
        P("seq", None),
        P("seq", None),
        P("seq"),
        P(),
        P(None, None, "segment"),
        P(None, "segment"),
        P("segment", None),
        P(),
        P(),
    )
    return jax.shard_map(
        on_device, mesh=mesh, in_specs=placed, out_specs=P("seq", "segment"), check_vma=False
    )
```
